32 devices in a mesh: depth: 4 (over y, x), au: 4 (over z), vert: 2 (over core).
Axes of the slice: x: 2, y: 2, z: 4, core: 2. Of those that a mesh axis runs over, the one named last changes fastest.
Arguments:
- density: float32 [64, 512, 256], P('depth', 'au', 'vert'), may hold values from 0.3 to 3
- image_cotangent: float32 [2, 512, 256], P(None, 'au', 'vert'), may hold values from -6 to 6
- shear_rows: int32 [64], P('depth'), may hold values from -16 to 16, as said below
- shear_cols: int32 [64], P('depth'), may hold values from -16 to 16, as said below
- velocity_code: int32 [2, 64, 512, 256], P(None, 'depth', 'au', 'vert'), may hold values from 0 to 26
- limiter: int32 [2, 64, 512, 256], P(None, 'depth', 'au', 'vert'), may hold values 0 or 1
Outputs:
- density_cotangent: float32 [64, 512, 256], P('depth', 'au', 'vert')
The draws below stay inside these ranges and needn't reach their ends.
Inputs may be any that keep to these rules, and one draw needn't show every extreme that they name: `shear_rows`: both values -16 and 16 occur in every draw. `shear_cols`: both values -16 and 16 occur in every draw.
All inputs are finite; a program needn't handle non-finite values. No bound on the sum of `limiter` on one device may be relied on, other than what follows from the above.
Results may differ from the reference program's by a relative error of at most 0.0003.
Values sent between devices are 32-bit elements; how exact they have to be, the bound alone decides.
A program may use at most 64 MiB of HBM per device.

```python
import math
import jax
import jax.numpy as jnp
from jax import lax

SHEAR = 16
STEPS = 2
NZ = 64
NU = 512
NV = 256


def shear_ramp(key, flip):
    slices = jnp.arange(NZ, dtype=jnp.int32)
    ramp = slices * (2 * SHEAR + 1) // NZ - SHEAR
    jitter = jax.random.randint(key, (NZ,), -2, 3, dtype=jnp.int32)
    values = jnp.clip(ramp + jitter, -SHEAR, SHEAR)
    values = jnp.where(slices == 0, -SHEAR, jnp.where(slices == NZ - 1, SHEAR, values))
    return (values * flip).astype(jnp.int32)


def draw_shear_rows(key, part):
    return shear_ramp(jax.random.fold_in(key, 11), 1)


def draw_shear_cols(key, part):
    return shear_ramp(jax.random.fold_in(key, 23), -1)


def touch_ends(values, stream_key, least, high):
    index_at = [jax.random.randint(jax.random.fold_in(stream_key, axis), (), 0, length) for axis, length in enumerate(values.shape)]
    main_axis = values.shape.index(max(values.shape))
    next_to = index_at[:main_axis] + [(index_at[main_axis] + 1) % values.shape[main_axis]] + index_at[main_axis + 1:]
    return values.at[tuple(index_at)].set(least).at[tuple(next_to)].set(high)


def block_levels(rng, dims, pieces, low, largest):
    level = 1.0
    for position, shards_of in pieces:
        heights = jax.random.uniform(jax.random.fold_in(jax.random.fold_in(rng, 6), position), (shards_of,), jnp.float32, low / len(pieces), largest / len(pieces))
        level = level * jnp.repeat(jnp.exp(heights), dims[position] // shards_of).reshape((-1,) + (1,) * (len(dims) - 1 - position))
    return level


def normal_values(key, dims, scale, bound, shards=(), kind=jnp.bfloat16):
    gain = block_levels(key, dims, shards, -0.22, 0.18) if shards else 1.0
    entries = jax.random.normal(key, dims, jnp.float32) * scale * gain
    return jnp.minimum(jnp.maximum(entries, -bound), bound).astype(kind)


def setup_inputs(seed: int = 0) -> dict:
    key_list = jax.random.split(jax.random.key(seed), 7)
    density = jnp.clip(jnp.exp(math.log(3.0) - 2.3025851 * jax.random.uniform(key_list[0], (NZ, NU, NV), jnp.float32) ** block_levels(key_list[0], (NZ, NU, NV), ((0, 4), (1, 4), (2, 2)), -0.2, 0.2)), 0.3, 3.0)
    image_cotangent = normal_values(key_list[1], (2, NU, NV), 1.0, 6.0, ((1, 4), (2, 2)), jnp.float32)
    shear_rows = draw_shear_rows(jax.random.fold_in(key_list[6], 71), 0)
    shear_cols = draw_shear_cols(jax.random.fold_in(key_list[6], 71), 0)
    velocity_code = touch_ends(jax.random.randint(key_list[4], (STEPS, NZ, NU, NV), 0, 27), jax.random.fold_in(key_list[4], 1), 0, 26).astype(jnp.int32)
    limiter = touch_ends((jax.random.randint(key_list[5], (STEPS, NZ, NU, NV), 0, 4) < 1).astype(jnp.int32), jax.random.fold_in(key_list[5], 1), 0, 1)
    return dict(density=density, image_cotangent=image_cotangent, shear_rows=shear_rows, shear_cols=shear_cols, velocity_code=velocity_code, limiter=limiter)


OPTICAL = 1.7
FRACTIONS = (0.3, 0.6, 0.45)


def shear_take(volume, offsets, axis_dim):
    pads = [(0, 0), (0, 0), (0, 0)]
    pads[axis_dim] = (SHEAR, SHEAR)
    padded = jnp.pad(volume, pads)
    length = volume.shape[axis_dim]

    def sample(plane, offset):
        return lax.dynamic_slice_in_dim(plane, (SHEAR + offset).astype(jnp.int32), length, axis_dim - 1)

    return jax.vmap(sample)(padded, offsets)


def column_gradient(views, cotangent, delta):
    optical = delta * views
    running = jnp.cumsum(optical, axis=0)
    transmit = jnp.exp(-(running - optical))
    opacity = -jnp.expm1(-optical)
    weighted = transmit * opacity * views
    light_sum = jnp.cumsum(weighted, axis=0)
    later_light = light_sum[-1:] - light_sum
    return cotangent[None] * (transmit * (jnp.exp(-optical) * views + opacity / delta) - later_light)


def sweep(values, offset, axis_dim, frac, direction):
    pads = [(0, 0), (0, 0), (0, 0)]
    pads[axis_dim] = (2, 2)
    padded = jnp.pad(values, pads)
    length = values.shape[axis_dim]

    def moved(distance):
        return lax.slice_in_dim(padded, 2 + distance, 2 + distance + length, axis=axis_dim)

    result = None
    for candidate in (-1, 0, 1):
        value = (1.0 - frac) * moved(direction * candidate) + frac * moved(direction * (candidate + 1))
        result = value if result is None else jnp.where(offset == candidate, value, result)
    return result


def adjoint_push(values, offsets, direction):
    values = sweep(values, offsets[2], 2, FRACTIONS[2], direction)
    values = sweep(values, offsets[1], 1, FRACTIONS[1], direction)
    return sweep(values, offsets[0], 0, FRACTIONS[0], direction)


def reference(density, image_cotangent, shear_rows, shear_cols, velocity_code, limiter):
    delta = OPTICAL / NZ
    grad_rows = column_gradient(shear_take(density, shear_rows, 1), image_cotangent[0], delta)
    grad_cols = column_gradient(shear_take(density, shear_cols, 2), image_cotangent[1], delta)
    cotangent = shear_take(grad_rows, -shear_rows, 1) + shear_take(grad_cols, -shear_cols, 2)
    for index in range(STEPS - 1, -1, -1):
        code = velocity_code[index]
        offsets = (code % 3 - 1, (code // 3) % 3 - 1, code // 9 - 1)
        kept = 0.5 * (1 - limiter[index]).astype(jnp.float32) * cotangent
        hat_grad = cotangent - adjoint_push(kept, offsets, -1)
        cotangent = kept + adjoint_push(hat_grad, offsets, 1)
    return cotangent
```

```python
import functools

import jax
import jax.numpy as jnp
from jax import lax
from jax.experimental import pallas as pl
from jax.experimental.pallas import tpu as pltpu
from jax.sharding import PartitionSpec as P

SHEAR = 16
OPTICAL = 1.7
FRACTIONS = (0.3, 0.6, 0.45)
MESH = pl.DeviceIdType.MESH
HALO = 8
ROWS = 32


def remote(src, dst, send, recv, device):
    return pltpu.make_async_remote_copy(
        src_ref=src, dst_ref=dst, send_sem=send, recv_sem=recv, device_id=device, device_id_type=MESH
    )


def blend(taps, low, mid, frac):
    first = jnp.where(low, taps[0], jnp.where(mid, taps[1], taps[2]))
    second = jnp.where(low, taps[1], jnp.where(mid, taps[2], taps[3]))
    return (1.0 - frac) * first + frac * second


def masks_v(code):
    return code < 9, code < 18


def rest_u(code):
    return code - jnp.where(code < 9, 0, jnp.where(code < 18, 9, 18))


def masks_u(code):
    rest = rest_u(code)
    return rest < 3, rest < 6


def masks_z(code):
    rest = rest_u(code)
    rest = rest - jnp.where(rest < 3, 0, jnp.where(rest < 6, 3, 6))
    return rest < 1, rest < 2


def kernel(
    sizes, rows_ref, cols_ref, dens, image, codes, limits, out,
    brick, code, lim, img, xs, es, ts, grad0, grad1, cots, kepts, tu, tz, res,
    tl, gath, pr, back,
    ds_s, ds_r, dh_s, dh_r, lc, cs_s, cs_r, is_s, is_r, ga_s, ga_r, bk_s, bk_r,
    gh_s, gh_r, us, ur, zs, zr, os_s, os_r,
):
    D, A, V = sizes
    nz, nu, nv = dens.shape
    steps = codes.shape[0]
    nub, nvf = nu // V, nv * V
    d, a, c = lax.axis_index("depth"), lax.axis_index("au"), lax.axis_index("vert")
    p = a * V + c
    has_prev, has_next = p > 0, p < A * V - 1
    prev = {"au": lax.div(p - 1 + V, V) - 1, "vert": lax.rem(p - 1 + V, V)}
    nxt = {"au": lax.div(p + 1, V), "vert": lax.rem(p + 1, V)}
    delta = OPTICAL / (nz * D)

    barrier = pltpu.get_barrier_semaphore()

    def greet(device):
        pl.semaphore_signal(barrier, inc=1, device_id=device, device_id_type=MESH)

    for k in range(1, V):
        greet({"vert": lax.rem(c + k, V)})
    for k in range(1, D):
        greet({"depth": lax.rem(d + k, D)})

    @pl.when(a > 0)
    def _():
        for w in range(V):
            greet({"au": a - 1, "vert": w})

    @pl.when(a < A - 1)
    def _():
        for w in range(V):
            greet({"au": a + 1, "vert": w})

    beside = jnp.minimum(a, 1) + jnp.minimum(A - 1 - a, 1)
    pl.semaphore_wait(barrier, V - 1 + D - 1 + V * beside)

    def cut(w):
        return max(0, w * nub - SHEAR), min(nu, w * nub + nub + SHEAR)

    def lanes(w):
        return pl.ds(w * nv, nv)

    def to_brick(w, frm):
        lo, hi = cut(w)
        at = lo - w * nub + SHEAR
        return dens.at[:, lo:hi, :], brick.at[:, at:at + hi - lo, lanes(frm)]

    def block(source, target, w, frm):
        return source.at[..., w * nub:(w + 1) * nub, :], target.at[..., lanes(frm)]

    def each_core(action):
        for mine in range(V):
            pl.when(c == mine)(functools.partial(action, mine))

    def inputs(mine):
        local = [pltpu.make_async_copy(*to_brick(mine, mine), lc.at[0])]
        local.append(pltpu.make_async_copy(*block(image, img, mine, mine), lc.at[1]))
        for s in range(steps):
            local.append(pltpu.make_async_copy(*block(codes.at[s], code.at[s], mine, mine), lc.at[2 + 2 * s]))
            local.append(pltpu.make_async_copy(*block(limits.at[s], lim.at[s], mine, mine), lc.at[3 + 2 * s]))
        return local

    def start_inputs(mine):
        @pl.when(a > 0)
        def _():
            remote(dens.at[:, :SHEAR, :], brick.at[:, SHEAR + nub:, lanes(mine)], dh_s.at[0], dh_r.at[0, mine],
                   {"au": a - 1, "vert": V - 1}).start()

        @pl.when(a < A - 1)
        def _():
            remote(dens.at[:, nu - SHEAR:, :], brick.at[:, :SHEAR, lanes(mine)], dh_s.at[1], dh_r.at[1, mine],
                   {"au": a + 1, "vert": 0}).start()

        others = [w for w in range(V) if w != mine]
        for w in others:
            remote(*to_brick(w, mine), ds_s.at[w], ds_r.at[mine], {"vert": w}).start()
        local = inputs(mine)
        for one in local:
            one.start()
        for w in others:
            remote(*block(image, img, w, mine), is_s.at[w], is_r.at[mine], {"vert": w}).start()
        for s in range(steps - 1, -1, -1):
            for w in others:
                remote(*block(limits.at[s], lim.at[s], w, mine), cs_s.at[s, 1, w], cs_r.at[s, 1, mine], {"vert": w}).start()
                remote(*block(codes.at[s], code.at[s], w, mine), cs_s.at[s, 0, w], cs_r.at[s, 0, mine], {"vert": w}).start()

    each_core(start_inputs)

    @pl.when(jnp.logical_not(has_prev))
    def _():
        brick[:, :SHEAR, :] = jnp.zeros((nz, SHEAR, nvf), jnp.float32)
        grad0[:, :SHEAR, :] = jnp.zeros((nz, SHEAR, nvf), jnp.float32)
        for e in range(2 * steps):
            tu[e, :, :HALO, :] = jnp.zeros((nz, HALO, nvf), jnp.float32)

    @pl.when(jnp.logical_not(has_next))
    def _():
        brick[:, SHEAR + nub:, :] = jnp.zeros((nz, SHEAR, nvf), jnp.float32)
        grad0[:, SHEAR + nub:, :] = jnp.zeros((nz, SHEAR, nvf), jnp.float32)
        for e in range(2 * steps):
            tu[e, :, HALO + nub:, :] = jnp.zeros((nz, HALO, nvf), jnp.float32)

    @pl.when(d == 0)
    def _():
        for e in range(2 * steps):
            tz[e, :2] = jnp.zeros((2, nub, nvf), jnp.float32)

    @pl.when(d == D - 1)
    def _():
        for e in range(2 * steps):
            tz[e, nz + 2:] = jnp.zeros((2, nub, nvf), jnp.float32)

    def wait_brick(mine):
        inputs(mine)[0].wait()
        for w in range(V):
            if w != mine:
                lo, hi = cut(mine)
                at = lo - mine * nub + SHEAR
                here = brick.at[:, at:at + hi - lo, lanes(w)]
                remote(here, here, ds_s.at[w], ds_r.at[w], {"vert": w}).wait_recv()
        if mine == V - 1:
            @pl.when(a < A - 1)
            def _():
                for w in range(V):
                    here = brick.at[:, SHEAR + nub:, lanes(w)]
                    remote(here, here, dh_s.at[0], dh_r.at[0, w], {"au": a + 1, "vert": w}).wait_recv()
        if mine == 0:
            @pl.when(a > 0)
            def _():
                for w in range(V):
                    here = brick.at[:, :SHEAR, lanes(w)]
                    remote(here, here, dh_s.at[1], dh_r.at[1, w], {"au": a - 1, "vert": w}).wait_recv()

    each_core(wait_brick)

    column = lax.broadcasted_iota(jnp.int32, (ROWS, nvf), 1)

    def moved(values, by):
        rolled = pltpu.roll(values, lax.rem(nvf - by, nvf), 1)
        at = column + by
        return jnp.where((at >= 0) & (at < nvf), rolled, 0.0)

    chunks = [(r, pl.ds(r, ROWS)) for r in range(0, nub, ROWS)]

    def shifted(ref, z, r, by):
        span = ROWS + 2 * SHEAR
        rows = ref[z, pl.ds(r, span), :]
        return pltpu.roll(rows, lax.rem(span - SHEAR - by, span), 0)[:ROWS]

    for view in range(2):
        for r, here in chunks:
            def ahead(z, carry, view=view, r=r, here=here):
                trans, light = carry
                if view == 0:
                    x = shifted(brick, z, r, rows_ref[z])
                else:
                    x = moved(brick[z, pl.ds(SHEAR + r, ROWS), :], cols_ref[z])
                e = jnp.exp(-delta * x)
                xs[view, z, here, :] = x
                es[view, z, here, :] = e
                ts[view, z, here, :] = trans
                return trans * e, light + trans * (1.0 - e) * x

            ones = jnp.ones((ROWS, nvf), jnp.float32)
            trans, light = lax.fori_loop(0, nz, ahead, (ones, jnp.zeros_like(ones)))
            tl[0, pl.ds(view * nub + r, ROWS), :] = trans
            tl[1, pl.ds(view * nub + r, ROWS), :] = light

    part = 2 * nub // D

    def at_part(k):
        return pl.ds(pl.multiple_of(k * part, part), part)

    def gather(k):
        peer = lax.rem(d + k, D)
        return remote(tl.at[:, at_part(peer), :], gath.at[d], ga_s.at[k], ga_r.at[k], {"depth": peer})

    for k in range(1, D):
        gather(k).start()
    gath[d] = tl[:, at_part(d), :]
    for k in range(1, D):
        here = gath.at[lax.rem(d - k + D, D)]
        remote(here, here, ga_s.at[k], ga_r.at[k], {"depth": lax.rem(d - k + D, D)}).wait_recv()
    run = jnp.ones((part, nvf), jnp.float32)
    for k in range(D):
        pr[k, 0] = run
        run = run * gath[k, 0]
    run = jnp.zeros((part, nvf), jnp.float32)
    for k in range(D - 1, -1, -1):
        pr[k, 1] = run
        run = gath[k, 1] + gath[k, 0] * run

    def give(k):
        peer = lax.rem(d + k, D)
        return remote(pr.at[peer], back.at[:, at_part(d), :], bk_s.at[k], bk_r.at[k], {"depth": peer})

    for k in range(1, D):
        give(k).start()
    back[:, at_part(d), :] = pr[d]

    def wait_image(mine):
        inputs(mine)[1].wait()
        for w in range(V):
            if w != mine:
                here = img.at[..., lanes(w)]
                remote(here, here, is_s.at[w], is_r.at[w], {"vert": w}).wait_recv()

    each_core(wait_image)
    for k in range(1, D):
        here = back.at[:, at_part(lax.rem(d - k + D, D)), :]
        remote(here, here, bk_s.at[k], bk_r.at[k], {"depth": lax.rem(d - k + D, D)}).wait_recv()

    def grad_up():
        return remote(grad0.at[:, SHEAR:2 * SHEAR, :], grad0.at[:, SHEAR + nub:, :], gh_s.at[0], gh_r.at[0], prev)

    def grad_down():
        return remote(grad0.at[:, nub:nub + SHEAR, :], grad0.at[:, :SHEAR, :], gh_s.at[1], gh_r.at[1], nxt)

    for view in range(2):
        for r, here in chunks:
            mine = pl.ds(view * nub + r, ROWS)
            before = back[0, mine, :]
            weight = img[view, here, :]
            later = before * tl[0, mine, :] * back[1, mine, :]

            def behind(k, later, view=view, r=r, here=here, before=before, weight=weight):
                z = nz - 1 - k
                x, e = xs[view, z, here, :], es[view, z, here, :]
                trans = before * ts[view, z, here, :]
                opacity = 1.0 - e
                grad = weight * (trans * (e * x + opacity * (1.0 / delta)) - later)
                if view == 0:
                    grad0[z, pl.ds(SHEAR + r, ROWS), :] = grad
                else:
                    grad1[z, here, :] = grad
                return later + trans * opacity * x

            lax.fori_loop(0, nz, behind, later)
        if view == 0:
            @pl.when(has_prev)
            def _():
                grad_up().start()

            @pl.when(has_next)
            def _():
                grad_down().start()

    def wait_codes(mine):
        for one in inputs(mine)[2:]:
            one.wait()
        for s in range(steps):
            for w in range(V):
                if w != mine:
                    for kind, target in ((0, code), (1, lim)):
                        here = target.at[s, ..., lanes(w)]
                        remote(here, here, cs_s.at[s, kind, w], cs_r.at[s, kind, w], {"vert": w}).wait_recv()

    each_core(wait_codes)

    @pl.when(has_next)
    def _():
        grad_up().wait_recv()

    @pl.when(has_prev)
    def _():
        grad_down().wait_recv()

    middle = nz // 2
    groups = ((0, 2), (nz - 2, nz), (2, middle), (middle, nz - 2))
    edges_first, edges_last = (0, 1, 2, 3), (2, 3, 0, 1)

    def u_up(e, g):
        lo, hi = groups[g]
        return remote(tu.at[e, lo:hi, HALO:2 * HALO, :], tu.at[e, lo:hi, HALO + nub:, :],
                      us.at[e, g, 0], ur.at[e, g, 0], prev)

    def u_down(e, g):
        lo, hi = groups[g]
        return remote(tu.at[e, lo:hi, nub:nub + HALO, :], tu.at[e, lo:hi, :HALO, :],
                      us.at[e, g, 1], ur.at[e, g, 1], nxt)

    def u_start(e, g):
        @pl.when(has_prev)
        def _():
            u_up(e, g).start()

        @pl.when(has_next)
        def _():
            u_down(e, g).start()

    def u_wait(e, g):
        @pl.when(has_next)
        def _():
            u_up(e, g).wait_recv()

        @pl.when(has_prev)
        def _():
            u_down(e, g).wait_recv()

    def z_up(e):
        after = 1 + e % 2
        return remote(tz.at[e, 2:2 + after], tz.at[e, nz + 2:nz + 2 + after], zs.at[e, 0], zr.at[e, 0], {"depth": d - 1})

    def z_down(e):
        before = 2 - e % 2
        return remote(tz.at[e, nz + 2 - before:nz + 2], tz.at[e, 2 - before:2], zs.at[e, 1], zr.at[e, 1], {"depth": d + 1})

    def z_start(e):
        @pl.when(d > 0)
        def _():
            z_up(e).start()

        @pl.when(d < D - 1)
        def _():
            z_down(e).start()

    def z_wait(e):
        @pl.when(d < D - 1)
        def _():
            z_up(e).wait_recv()

        @pl.when(d > 0)
        def _():
            z_down(e).wait_recv()

    def over(g, body):
        lo, hi = groups[g]

        def one(z, carry):
            for r, here in chunks:
                body(z, r, here)
            return carry

        lax.fori_loop(lo, hi, one, 0)

    def v_sweep(values, cells, sign):
        taps = [values if n == 0 else moved(values, sign * n) for n in (-1, 0, 1, 2)]
        return blend(taps, *masks_v(cells), FRACTIONS[2])

    def open_step(n, z, r, here, cot):
        s = steps - 1 - n
        cots[n, z, here, :] = cot
        kept = jnp.where(lim[s, z, here, :] == 0, 0.5 * cot, 0.0)
        kepts[n, z, here, :] = kept
        tu[2 * n, z, pl.ds(HALO + r, ROWS), :] = v_sweep(kept, code[s, z, here, :], -1)

    def first(z, r, here):
        cot = shifted(grad0, z, r, -rows_ref[z]) + moved(grad1[z, here, :], -cols_ref[z])
        open_step(0, z, r, here, cot)

    for g in edges_first:
        over(g, first)
        u_start(0, g)

    def out_copy(mine, w, g):
        lo, hi = groups[g]
        return res.at[lo:hi, :, lanes(w)], out.at[lo:hi, mine * nub:(mine + 1) * nub, :]

    def out_start(g, mine):
        pltpu.make_async_copy(*out_copy(mine, mine, g), os_s.at[g, mine]).start()
        for w in range(V):
            if w != mine:
                remote(*out_copy(mine, w, g), os_s.at[g, w], os_r.at[g, mine], {"vert": w}).start()

    for n in range(steps):
        s = steps - 1 - n
        for half in range(2):
            e, sign = 2 * n + half, 2 * half - 1

            def u_body(z, r, here, e=e, sign=sign, s=s):
                taps = [tu[e, z, pl.ds(HALO + r + sign * k, ROWS), :] for k in (-1, 0, 1, 2)]
                tz[e, z + 2, here, :] = blend(taps, *masks_u(code[s, z, here, :]), FRACTIONS[1])

            for i, g in enumerate(edges_first):
                u_wait(e, g)
                over(g, u_body)
                if i == 1:
                    z_start(e)

            def z_body(z, r, here, e=e, sign=sign, s=s, n=n, half=half):
                cells = code[s, z, here, :]
                taps = [tz[e, z + 2 + sign * k, here, :] for k in (-1, 0, 1, 2)]
                swept = blend(taps, *masks_z(cells), FRACTIONS[0])
                if half == 0:
                    hat = cots[n, z, here, :] - swept
                    tu[e + 1, z, pl.ds(HALO + r, ROWS), :] = v_sweep(hat, cells, 1)
                elif n < steps - 1:
                    open_step(n + 1, z, r, here, kepts[n, z, here, :] + swept)
                else:
                    res[z, here, :] = kepts[n, z, here, :] + swept

            for i, g in enumerate(edges_last):
                if i == 2:
                    z_wait(e)
                over(g, z_body)
                if e + 1 < 2 * steps:
                    u_start(e + 1, g)
                else:
                    each_core(functools.partial(out_start, g))

    def drain(mine):
        for g in range(len(groups)):
            pltpu.make_async_copy(*out_copy(mine, mine, g), os_s.at[g, mine]).wait()
            lo, hi = groups[g]
            for w in range(V):
                if w != mine:
                    remote(*out_copy(mine, w, g), os_s.at[g, w], os_r.at[g, mine], {"vert": w}).wait_send()
                    here = out.at[lo:hi, w * nub:(w + 1) * nub, :]
                    remote(here, here, os_s.at[g, w], os_r.at[g, w], {"vert": w}).wait_recv()
        for w in range(V):
            if w != mine:
                remote(*to_brick(w, mine), ds_s.at[w], ds_r.at[mine], {"vert": w}).wait_send()
                remote(*block(image, img, w, mine), is_s.at[w], is_r.at[mine], {"vert": w}).wait_send()
                for s in range(steps):
                    remote(*block(codes.at[s], code.at[s], w, mine), cs_s.at[s, 0, w], cs_r.at[s, 0, mine], {"vert": w}).wait_send()
                    remote(*block(limits.at[s], lim.at[s], w, mine), cs_s.at[s, 1, w], cs_r.at[s, 1, mine], {"vert": w}).wait_send()

        @pl.when(a > 0)
        def _():
            remote(dens.at[:, :SHEAR, :], brick.at[:, SHEAR + nub:, lanes(mine)], dh_s.at[0], dh_r.at[0, mine],
                   {"au": a - 1, "vert": V - 1}).wait_send()

        @pl.when(a < A - 1)
        def _():
            remote(dens.at[:, nu - SHEAR:, :], brick.at[:, :SHEAR, lanes(mine)], dh_s.at[1], dh_r.at[1, mine],
                   {"au": a + 1, "vert": 0}).wait_send()

    each_core(drain)
    for k in range(1, D):
        gather(k).wait_send()
        give(k).wait_send()

    @pl.when(has_prev)
    def _():
        grad_up().wait_send()
        for e in range(2 * steps):
            for g in range(len(groups)):
                u_up(e, g).wait_send()

    @pl.when(has_next)
    def _():
        grad_down().wait_send()
        for e in range(2 * steps):
            for g in range(len(groups)):
                u_down(e, g).wait_send()

    @pl.when(d > 0)
    def _():
        for e in range(2 * steps):
            z_up(e).wait_send()

    @pl.when(d < D - 1)
    def _():
        for e in range(2 * steps):
            z_down(e).wait_send()


def per_device(sizes, density, image_cotangent, shear_rows, shear_cols, velocity_code, limiter):
    D, A, V = sizes
    nz, nu, nv = density.shape
    steps = velocity_code.shape[0]
    nub, nvf = nu // V, nv * V
    f32, i32 = jnp.float32, jnp.int32
    vmem, dma = pltpu.VMEM, pltpu.SemaphoreType.DMA
    part = 2 * nub // D
    scratch = [
        vmem((nz, nub + 2 * SHEAR, nvf), f32),
        vmem((steps, nz, nub, nvf), i32),
        vmem((steps, nz, nub, nvf), i32),
        vmem((2, nub, nvf), f32),
        vmem((2, nz, nub, nvf), f32),
        vmem((2, nz, nub, nvf), f32),
        vmem((2, nz, nub, nvf), f32),
        vmem((nz, nub + 2 * SHEAR, nvf), f32),
        vmem((nz, nub, nvf), f32),
        vmem((steps, nz, nub, nvf), f32),
        vmem((steps, nz, nub, nvf), f32),
        vmem((2 * steps, nz, nub + 2 * HALO, nvf), f32),
        vmem((2 * steps, nz + 4, nub, nvf), f32),
        vmem((nz, nub, nvf), f32),
        vmem((2, 2 * nub, nvf), f32),
        vmem((D, 2, part, nvf), f32),
        vmem((D, 2, part, nvf), f32),
        vmem((2, 2 * nub, nvf), f32),
        dma((V,)), dma((V,)), dma((2,)), dma((2, V)), dma((2 + 2 * steps,)),
        dma((steps, 2, V)), dma((steps, 2, V)), dma((V,)), dma((V,)),
        dma((D,)), dma((D,)), dma((D,)), dma((D,)),
        dma((2,)), dma((2,)),
        dma((2 * steps, 4, 2)), dma((2 * steps, 4, 2)),
        dma((2 * steps, 2)), dma((2 * steps, 2)),
        dma((4, V)), dma((4, V)),
    ]
    smem = pl.BlockSpec(memory_space=pltpu.SMEM)
    far = pl.BlockSpec(memory_space=pl.ANY)
    return pl.pallas_call(
        functools.partial(kernel, sizes),
        out_shape=jax.ShapeDtypeStruct(density.shape, f32),
        in_specs=[smem, smem, far, far, far, far],
        out_specs=far,
        scratch_shapes=scratch,
        compiler_params=pltpu.CompilerParams(
            collective_id=0, has_side_effects=True, vmem_limit_bytes=56 * 1024 * 1024
        ),
    )(shear_rows, shear_cols, density, image_cotangent, velocity_code, limiter)


def solution(mesh):
    placed = (
        P("depth", "au", "vert"),
        P(None, "au", "vert"),
        P("depth"),
        P("depth"),
        P(None, "depth", "au", "vert"),
        P(None, "depth", "au", "vert"),
    )
    sizes = tuple(mesh.shape[name] for name in ("depth", "au", "vert"))
    return jax.shard_map(
        functools.partial(per_device, sizes), mesh=mesh, in_specs=placed,
        out_specs=P("depth", "au", "vert"), check_vma=False,
    )
```

```python
import functools

import jax
import jax.numpy as jnp
from jax import lax
from jax.experimental import pallas as pl
from jax.experimental.pallas import tpu as pltpu
from jax.sharding import PartitionSpec as P

SHEAR = 16
OPTICAL = 1.7
FRACTIONS = (0.3, 0.6, 0.45)
MESH = pl.DeviceIdType.MESH
HALO = 8
ROWS = 32


def remote(src, dst, send, recv, device):
    return pltpu.make_async_remote_copy(
        src_ref=src, dst_ref=dst, send_sem=send, recv_sem=recv, device_id=device, device_id_type=MESH
    )


def blend(taps, low, mid, frac):
    first = jnp.where(low, taps[0], jnp.where(mid, taps[1], taps[2]))
    second = jnp.where(low, taps[1], jnp.where(mid, taps[2], taps[3]))
    return (1.0 - frac) * first + frac * second


def masks_u(rest):
    return rest < 3, rest < 6


def masks_z(rest):
    return rest < 1, rest < 2


def kernel(
    sizes, rows_ref, cols_ref, dens, image, codes, limits, out,
    brick, code, lim, img, xs, es, ts, grad0, grad1, cots, kepts, tu, tz, res,
    tl, gath, pr, back, codeu, codez,
    ds_s, ds_r, dh_s, dh_r, lc, cs_s, cs_r, is_s, is_r, ga_s, ga_r, bk_s, bk_r,
    gh_s, gh_r, us, ur, zs, zr, os_s, os_r,
):
    D, A, V = sizes
    nz, nu, nv = dens.shape
    steps = codes.shape[0]
    nub, nvf = nu // V, nv * V
    d, a, c = lax.axis_index("depth"), lax.axis_index("au"), lax.axis_index("vert")
    p = a * V + c
    has_prev, has_next = p > 0, p < A * V - 1
    prev = {"au": lax.div(p - 1 + V, V) - 1, "vert": lax.rem(p - 1 + V, V)}
    nxt = {"au": lax.div(p + 1, V), "vert": lax.rem(p + 1, V)}
    delta = OPTICAL / (nz * D)

    barrier = pltpu.get_barrier_semaphore()

    def greet(device):
        pl.semaphore_signal(barrier, inc=1, device_id=device, device_id_type=MESH)

    for k in range(1, V):
        greet({"vert": lax.rem(c + k, V)})
    for k in range(1, D):
        greet({"depth": lax.rem(d + k, D)})

    @pl.when(a > 0)
    def _():
        for w in range(V):
            greet({"au": a - 1, "vert": w})

    @pl.when(a < A - 1)
    def _():
        for w in range(V):
            greet({"au": a + 1, "vert": w})

    beside = jnp.minimum(a, 1) + jnp.minimum(A - 1 - a, 1)
    pl.semaphore_wait(barrier, V - 1 + D - 1 + V * beside)

    def cut(w):
        return max(0, w * nub - SHEAR), min(nu, w * nub + nub + SHEAR)

    def lanes(w):
        return pl.ds(w * nv, nv)

    def to_brick(w, frm):
        lo, hi = cut(w)
        at = lo - w * nub + SHEAR
        return dens.at[:, lo:hi, :], brick.at[:, at:at + hi - lo, lanes(frm)]

    def block(source, target, w, frm):
        return source.at[..., w * nub:(w + 1) * nub, :], target.at[..., lanes(frm)]

    def each_core(action):
        for mine in range(V):
            pl.when(c == mine)(functools.partial(action, mine))

    def inputs(mine):
        local = [pltpu.make_async_copy(*to_brick(mine, mine), lc.at[0])]
        local.append(pltpu.make_async_copy(*block(image, img, mine, mine), lc.at[1]))
        for s in range(steps):
            local.append(pltpu.make_async_copy(*block(codes.at[s], code.at[s], mine, mine), lc.at[2 + 2 * s]))
            local.append(pltpu.make_async_copy(*block(limits.at[s], lim.at[s], mine, mine), lc.at[3 + 2 * s]))
        return local

    def start_inputs(mine):
        @pl.when(a > 0)
        def _():
            remote(dens.at[:, :SHEAR, :], brick.at[:, SHEAR + nub:2 * SHEAR + nub, lanes(mine)], dh_s.at[0], dh_r.at[0, mine],
                   {"au": a - 1, "vert": V - 1}).start()

        @pl.when(a < A - 1)
        def _():
            remote(dens.at[:, nu - SHEAR:, :], brick.at[:, :SHEAR, lanes(mine)], dh_s.at[1], dh_r.at[1, mine],
                   {"au": a + 1, "vert": 0}).start()

        others = [w for w in range(V) if w != mine]
        for w in others:
            remote(*to_brick(w, mine), ds_s.at[w], ds_r.at[mine], {"vert": w}).start()
        local = inputs(mine)
        for one in local:
            one.start()
        for w in others:
            remote(*block(image, img, w, mine), is_s.at[w], is_r.at[mine], {"vert": w}).start()
        for s in range(steps - 1, -1, -1):
            for w in others:
                remote(*block(limits.at[s], lim.at[s], w, mine), cs_s.at[s, 1, w], cs_r.at[s, 1, mine], {"vert": w}).start()
                remote(*block(codes.at[s], code.at[s], w, mine), cs_s.at[s, 0, w], cs_r.at[s, 0, mine], {"vert": w}).start()

    each_core(start_inputs)

    brick[:, 2 * SHEAR + nub:, :] = jnp.zeros((nz, 8, nvf), jnp.float32)
    grad0[:, 2 * SHEAR + nub:, :] = jnp.zeros((nz, 8, nvf), jnp.float32)

    @pl.when(jnp.logical_not(has_prev))
    def _():
        brick[:, :SHEAR, :] = jnp.zeros((nz, SHEAR, nvf), jnp.float32)
        grad0[:, :SHEAR, :] = jnp.zeros((nz, SHEAR, nvf), jnp.float32)
        for e in range(2 * steps):
            tu[e, :, :HALO, :] = jnp.zeros((nz, HALO, nvf), jnp.float32)

    @pl.when(jnp.logical_not(has_next))
    def _():
        brick[:, SHEAR + nub:2 * SHEAR + nub, :] = jnp.zeros((nz, SHEAR, nvf), jnp.float32)
        grad0[:, SHEAR + nub:2 * SHEAR + nub, :] = jnp.zeros((nz, SHEAR, nvf), jnp.float32)
        for e in range(2 * steps):
            tu[e, :, HALO + nub:, :] = jnp.zeros((nz, HALO, nvf), jnp.float32)

    @pl.when(d == 0)
    def _():
        for e in range(2 * steps):
            tz[e, :2] = jnp.zeros((2, nub, nvf), jnp.float32)

    @pl.when(d == D - 1)
    def _():
        for e in range(2 * steps):
            tz[e, nz + 2:] = jnp.zeros((2, nub, nvf), jnp.float32)

    def wait_brick(mine):
        inputs(mine)[0].wait()
        for w in range(V):
            if w != mine:
                lo, hi = cut(mine)
                at = lo - mine * nub + SHEAR
                here = brick.at[:, at:at + hi - lo, lanes(w)]
                remote(here, here, ds_s.at[w], ds_r.at[w], {"vert": w}).wait_recv()
        if mine == V - 1:
            @pl.when(a < A - 1)
            def _():
                for w in range(V):
                    here = brick.at[:, SHEAR + nub:2 * SHEAR + nub, lanes(w)]
                    remote(here, here, dh_s.at[0], dh_r.at[0, w], {"au": a + 1, "vert": w}).wait_recv()
        if mine == 0:
            @pl.when(a > 0)
            def _():
                for w in range(V):
                    here = brick.at[:, :SHEAR, lanes(w)]
                    remote(here, here, dh_s.at[1], dh_r.at[1, w], {"au": a - 1, "vert": w}).wait_recv()

    each_core(wait_brick)

    lane = lax.broadcasted_iota(jnp.int32, (ROWS, nv), 1)
    row = lax.broadcasted_iota(jnp.int32, (8, nvf), 0)
    nothing = jnp.zeros((ROWS, nv), jnp.float32)

    def tiles(values):
        return [nothing] + [values[:, w * nv:(w + 1) * nv] for w in range(V)] + [nothing]

    def joined(parts):
        return jnp.concatenate(parts, axis=1)

    def tap(parts, by):
        turned = [pltpu.roll(one, (-by) % nv, 1) for one in parts[1:-1]]
        turned = [nothing] + turned + [nothing]
        if by > 0:
            inside = lane < nv - by
            return [jnp.where(inside, turned[w], turned[w + 1]) for w in range(1, V + 1)]
        inside = lane >= -by
        return [jnp.where(inside, turned[w], turned[w - 1]) for w in range(1, V + 1)]

    def moved(values, by):
        turned = [pltpu.roll(one, lax.rem(nv - by, nv), 1) for one in tiles(values)[1:-1]]
        turned = [nothing] + turned + [nothing]
        at = lane + by
        return joined([
            jnp.where(at < 0, turned[w - 1], jnp.where(at < nv, turned[w], turned[w + 1])) for w in range(1, V + 1)
        ])

    chunks = [(r, pl.ds(r, ROWS)) for r in range(0, nub, ROWS)]

    def shifted(ref, z, r, by):
        span = ROWS + 2 * SHEAR
        rows = ref[z, pl.ds(r, span), :]
        return pltpu.roll(rows, lax.rem(span - SHEAR - by, span), 0)[:ROWS]

    part = V * nub // D

    def at_part(k):
        return pl.ds(pl.multiple_of(k * part, part), part)

    def gather(view, k):
        peer = lax.rem(d + k, D)
        return remote(tl.at[view, :, at_part(peer), :], gath.at[view, d], ga_s.at[view, k], ga_r.at[view, k],
                      {"depth": peer})

    def give(view, k):
        peer = lax.rem(d + k, D)
        return remote(pr.at[view, peer], back.at[view, :, at_part(d), :], bk_s.at[view, k], bk_r.at[view, k],
                      {"depth": peer})

    def put(view, kind, r, values):
        for w in range(V):
            tl[view, kind, pl.ds(w * nub + r, ROWS), :] = values[:, w * nv:(w + 1) * nv]

    def get(ref, view, kind, r):
        return joined([ref[view, kind, pl.ds(w * nub + r, ROWS), :] for w in range(V)])

    for view in range(2):
        for r, here in chunks:
            def ahead(z, carry, view=view, r=r, here=here):
                trans, light = carry
                if view == 0:
                    x = shifted(brick, z, r, rows_ref[z])
                else:
                    x = moved(brick[z, pl.ds(SHEAR + r, ROWS), :], cols_ref[z])
                e = jnp.exp(-delta * x)
                xs[view, z, here, :] = x
                es[view, z, here, :] = e
                ts[view, z, here, :] = trans
                left = trans * e
                return left, light + (trans - left) * x

            def ahead_pair(k, carry, ahead=ahead):
                return ahead(2 * k + 1, ahead(2 * k, carry))

            ones = jnp.ones((ROWS, nvf), jnp.float32)
            trans, light = lax.fori_loop(0, nz // 2, ahead_pair, (ones, jnp.zeros_like(ones)))
            put(view, 0, r, trans)
            put(view, 1, r, light)
        for k in range(1, D):
            gather(view, k).start()
        gath[view, d] = tl[view, :, at_part(d), :]

    for view in range(2):
        for k in range(1, D):
            peer = lax.rem(d - k + D, D)
            here = gath.at[view, peer]
            remote(here, here, ga_s.at[view, k], ga_r.at[view, k], {"depth": peer}).wait_recv()
        run = jnp.ones((part, nv), jnp.float32)
        for k in range(D):
            pr[view, k, 0] = run
            run = run * gath[view, k, 0]
        run = jnp.zeros((part, nv), jnp.float32)
        for k in range(D - 1, -1, -1):
            pr[view, k, 1] = run
            run = gath[view, k, 1] + gath[view, k, 0] * run
        for k in range(1, D):
            give(view, k).start()
        back[view, :, at_part(d), :] = pr[view, d]

    def wait_codes(mine):
        for one in inputs(mine)[2:]:
            one.wait()
        for s in range(steps):
            for w in range(V):
                if w != mine:
                    for kind, target in ((0, code), (1, lim)):
                        here = target.at[s, ..., lanes(w)]
                        remote(here, here, cs_s.at[s, kind, w], cs_r.at[s, kind, w], {"vert": w}).wait_recv()

    def decode(s):
        def one(z, carry):
            for r, here in chunks:
                cells = code[s, z, here, :]
                rest = cells - jnp.where(cells < 9, 0, jnp.where(cells < 18, 9, 18))
                codeu[s, z, here, :] = rest
                codez[s, z, here, :] = rest - jnp.where(rest < 3, 0, jnp.where(rest < 6, 3, 6))
            return carry

        lax.fori_loop(0, nz, one, 0)

    each_core(wait_codes)
    decode(steps - 1)

    def wait_image(mine):
        inputs(mine)[1].wait()
        for w in range(V):
            if w != mine:
                here = img.at[..., lanes(w)]
                remote(here, here, is_s.at[w], is_r.at[w], {"vert": w}).wait_recv()

    each_core(wait_image)
    def grad_up():
        return remote(grad0.at[:, SHEAR:2 * SHEAR, :], grad0.at[:, SHEAR + nub:2 * SHEAR + nub, :], gh_s.at[0], gh_r.at[0], prev)

    def grad_down():
        return remote(grad0.at[:, nub:nub + SHEAR, :], grad0.at[:, :SHEAR, :], gh_s.at[1], gh_r.at[1], nxt)

    for view in range(2):
        for k in range(1, D):
            peer = lax.rem(d - k + D, D)
            here = back.at[view, :, at_part(peer), :]
            remote(here, here, bk_s.at[view, k], bk_r.at[view, k], {"depth": peer}).wait_recv()
        for r, here in chunks:
            before = get(back, view, 0, r)
            weight = img[view, here, :]
            later = before * get(tl, view, 0, r) * get(back, view, 1, r)

            def behind(z, later, view=view, r=r, here=here, before=before, weight=weight):
                x, e = xs[view, z, here, :], es[view, z, here, :]
                trans = before * ts[view, z, here, :]
                left = trans * e
                lost = trans - left
                grad = weight * (left * x + lost * (1.0 / delta) - later)
                if view == 0:
                    grad0[z, pl.ds(SHEAR + r, ROWS), :] = grad
                else:
                    grad1[z, here, :] = grad
                return later + lost * x

            def behind_pair(k, later, behind=behind):
                return behind(nz - 2 - 2 * k, behind(nz - 1 - 2 * k, later))

            lax.fori_loop(0, nz // 2, behind_pair, later)
            if view == 0 and r == 0:
                @pl.when(has_prev)
                def _():
                    grad_up().start()
        if view == 0:
            @pl.when(has_next)
            def _():
                grad_down().start()

    for s in range(steps - 1):
        decode(s)

    @pl.when(has_next)
    def _():
        grad_up().wait_recv()

    @pl.when(has_prev)
    def _():
        grad_down().wait_recv()

    middle = nz // 2
    groups = ((0, 2), (nz - 2, nz), (2, middle), (middle, nz - 2))
    edges_first, edges_last = (0, 1, 2, 3), (2, 3, 0, 1)

    def u_up(e, g):
        lo, hi = groups[g]
        return remote(tu.at[e, lo:hi, HALO:2 * HALO, :], tu.at[e, lo:hi, HALO + nub:, :],
                      us.at[e, g, 0], ur.at[e, g, 0], prev)

    def u_down(e, g):
        lo, hi = groups[g]
        return remote(tu.at[e, lo:hi, nub:nub + HALO, :], tu.at[e, lo:hi, :HALO, :],
                      us.at[e, g, 1], ur.at[e, g, 1], nxt)

    def u_start(e, g):
        @pl.when(has_prev)
        def _():
            u_up(e, g).start()

        @pl.when(has_next)
        def _():
            u_down(e, g).start()

    def u_wait(e, g):
        @pl.when(has_next)
        def _():
            u_up(e, g).wait_recv()

        @pl.when(has_prev)
        def _():
            u_down(e, g).wait_recv()

    def z_up(e):
        after = 1 + e % 2
        return remote(tz.at[e, 2:2 + after], tz.at[e, nz + 2:nz + 2 + after], zs.at[e, 0], zr.at[e, 0], {"depth": d - 1})

    def z_down(e):
        before = 2 - e % 2
        return remote(tz.at[e, nz + 2 - before:nz + 2], tz.at[e, 2 - before:2], zs.at[e, 1], zr.at[e, 1], {"depth": d + 1})

    def z_start(e):
        @pl.when(d > 0)
        def _():
            z_up(e).start()

        @pl.when(d < D - 1)
        def _():
            z_down(e).start()

    def z_wait(e):
        @pl.when(d < D - 1)
        def _():
            z_up(e).wait_recv()

        @pl.when(d > 0)
        def _():
            z_down(e).wait_recv()

    def over(g, body):
        lo, hi = groups[g]

        def two(k, carry):
            for z in (lo + 2 * k, lo + 2 * k + 1):
                for r, here in chunks:
                    body(z, r, here)
            return carry

        lax.fori_loop(0, (hi - lo) // 2, two, 0)

    def v_sweep(values, cells, sign):
        parts = tiles(values)
        taps = [parts[1:-1] if n == 0 else tap(parts, sign * n) for n in (-1, 0, 1, 2)]
        low, mid = cells < 9, cells < 18
        return joined([
            blend([one[w] for one in taps], low[:, w * nv:(w + 1) * nv], mid[:, w * nv:(w + 1) * nv], FRACTIONS[2])
            for w in range(V)
        ])

    def open_step(n, z, r, here, cot):
        s = steps - 1 - n
        cots[n, z, here, :] = cot
        kept = jnp.where(lim[s, z, here, :] == 0, 0.5 * cot, 0.0)
        kepts[n, z, here, :] = kept
        tu[2 * n, z, pl.ds(HALO + r, ROWS), :] = v_sweep(kept, code[s, z, here, :], -1)

    def first(z, r, here):
        cot = shifted(grad0, z, r, -rows_ref[z]) + moved(grad1[z, here, :], -cols_ref[z])
        open_step(0, z, r, here, cot)

    for g in edges_first:
        over(g, first)
        u_start(0, g)

    def out_copy(mine, w, g):
        lo, hi = groups[g]
        return res.at[lo:hi, :, lanes(w)], out.at[lo:hi, mine * nub:(mine + 1) * nub, :]

    def out_start(g, mine):
        pltpu.make_async_copy(*out_copy(mine, mine, g), os_s.at[g, mine]).start()
        for w in range(V):
            if w != mine:
                remote(*out_copy(mine, w, g), os_s.at[g, w], os_r.at[g, mine], {"vert": w}).start()

    for n in range(steps):
        s = steps - 1 - n
        for half in range(2):
            e, sign = 2 * n + half, 2 * half - 1

            def u_body(z, r, here, e=e, sign=sign, s=s):
                taps = [tu[e, z, pl.ds(HALO + r + sign * k, ROWS), :] for k in (-1, 0, 1, 2)]
                tz[e, z + 2, here, :] = blend(taps, *masks_u(codeu[s, z, here, :]), FRACTIONS[1])

            order = edges_first if e == 0 else (2, 0, 1, 3)
            for g in order:
                u_wait(e, g)
                over(g, u_body)
                if g == 1:
                    z_start(e)

            def z_body(z, r, here, e=e, sign=sign, s=s, n=n, half=half):
                cells = code[s, z, here, :]
                taps = [tz[e, z + 2 + sign * k, here, :] for k in (-1, 0, 1, 2)]
                swept = blend(taps, *masks_z(codez[s, z, here, :]), FRACTIONS[0])
                if half == 0:
                    hat = cots[n, z, here, :] - swept
                    tu[e + 1, z, pl.ds(HALO + r, ROWS), :] = v_sweep(hat, cells, 1)
                elif n < steps - 1:
                    open_step(n + 1, z, r, here, kepts[n, z, here, :] + swept)
                else:
                    res[z, here, :] = kepts[n, z, here, :] + swept

            for i, g in enumerate(edges_last):
                if i == 2:
                    z_wait(e)
                over(g, z_body)
                if e + 1 < 2 * steps:
                    u_start(e + 1, g)
                else:
                    each_core(functools.partial(out_start, g))

    def drain(mine):
        for g in range(len(groups)):
            pltpu.make_async_copy(*out_copy(mine, mine, g), os_s.at[g, mine]).wait()
            lo, hi = groups[g]
            for w in range(V):
                if w != mine:
                    remote(*out_copy(mine, w, g), os_s.at[g, w], os_r.at[g, mine], {"vert": w}).wait_send()
                    here = out.at[lo:hi, w * nub:(w + 1) * nub, :]
                    remote(here, here, os_s.at[g, w], os_r.at[g, w], {"vert": w}).wait_recv()
        for w in range(V):
            if w != mine:
                remote(*to_brick(w, mine), ds_s.at[w], ds_r.at[mine], {"vert": w}).wait_send()
                remote(*block(image, img, w, mine), is_s.at[w], is_r.at[mine], {"vert": w}).wait_send()
                for s in range(steps):
                    remote(*block(codes.at[s], code.at[s], w, mine), cs_s.at[s, 0, w], cs_r.at[s, 0, mine], {"vert": w}).wait_send()
                    remote(*block(limits.at[s], lim.at[s], w, mine), cs_s.at[s, 1, w], cs_r.at[s, 1, mine], {"vert": w}).wait_send()

        @pl.when(a > 0)
        def _():
            remote(dens.at[:, :SHEAR, :], brick.at[:, SHEAR + nub:2 * SHEAR + nub, lanes(mine)], dh_s.at[0], dh_r.at[0, mine],
                   {"au": a - 1, "vert": V - 1}).wait_send()

        @pl.when(a < A - 1)
        def _():
            remote(dens.at[:, nu - SHEAR:, :], brick.at[:, :SHEAR, lanes(mine)], dh_s.at[1], dh_r.at[1, mine],
                   {"au": a + 1, "vert": 0}).wait_send()

    each_core(drain)
    for view in range(2):
        for k in range(1, D):
            gather(view, k).wait_send()
            give(view, k).wait_send()

    @pl.when(has_prev)
    def _():
        grad_up().wait_send()
        for e in range(2 * steps):
            for g in range(len(groups)):
                u_up(e, g).wait_send()

    @pl.when(has_next)
    def _():
        grad_down().wait_send()
        for e in range(2 * steps):
            for g in range(len(groups)):
                u_down(e, g).wait_send()

    @pl.when(d > 0)
    def _():
        for e in range(2 * steps):
            z_up(e).wait_send()

    @pl.when(d < D - 1)
    def _():
        for e in range(2 * steps):
            z_down(e).wait_send()


def per_device(sizes, density, image_cotangent, shear_rows, shear_cols, velocity_code, limiter):
    D, A, V = sizes
    nz, nu, nv = density.shape
    steps = velocity_code.shape[0]
    nub, nvf = nu // V, nv * V
    f32, i32 = jnp.float32, jnp.int32
    vmem, dma = pltpu.VMEM, pltpu.SemaphoreType.DMA
    part = V * nub // D
    scratch = [
        vmem((nz, nub + 2 * SHEAR + 8, nvf), f32),
        vmem((steps, nz, nub, nvf), i32),
        vmem((steps, nz, nub, nvf), i32),
        vmem((2, nub, nvf), f32),
        vmem((2, nz, nub, nvf), f32),
        vmem((2, nz, nub, nvf), f32),
        vmem((2, nz, nub, nvf), f32),
        vmem((nz, nub + 2 * SHEAR + 8, nvf), f32),
        vmem((nz, nub, nvf), f32),
        vmem((steps, nz, nub, nvf), f32),
        vmem((steps, nz, nub, nvf), f32),
        vmem((2 * steps, nz, nub + 2 * HALO, nvf), f32),
        vmem((2 * steps, nz + 4, nub, nvf), f32),
        vmem((nz, nub, nvf), f32),
        vmem((2, 2, V * nub, nv), f32),
        vmem((2, D, 2, part, nv), f32),
        vmem((2, D, 2, part, nv), f32),
        vmem((2, 2, V * nub, nv), f32),
        vmem((steps, nz, nub, nvf), i32),
        vmem((steps, nz, nub, nvf), i32),
        dma((V,)), dma((V,)), dma((2,)), dma((2, V)), dma((2 + 2 * steps,)),
        dma((steps, 2, V)), dma((steps, 2, V)), dma((V,)), dma((V,)),
        dma((2, D)), dma((2, D)), dma((2, D)), dma((2, D)),
        dma((2,)), dma((2,)),
        dma((2 * steps, 4, 2)), dma((2 * steps, 4, 2)),
        dma((2 * steps, 2)), dma((2 * steps, 2)),
        dma((4, V)), dma((4, V)),
    ]
    smem = pl.BlockSpec(memory_space=pltpu.SMEM)
    far = pl.BlockSpec(memory_space=pl.ANY)
    return pl.pallas_call(
        functools.partial(kernel, sizes),
        out_shape=jax.ShapeDtypeStruct(density.shape, f32),
        in_specs=[smem, smem, far, far, far, far],
        out_specs=far,
        scratch_shapes=scratch,
        compiler_params=pltpu.CompilerParams(
            collective_id=0, has_side_effects=True, vmem_limit_bytes=56 * 1024 * 1024
        ),
    )(shear_rows, shear_cols, density, image_cotangent, velocity_code, limiter)


def solution(mesh):
    placed = (
        P("depth", "au", "vert"),
        P(None, "au", "vert"),
        P("depth"),
        P("depth"),
        P(None, "depth", "au", "vert"),
        P(None, "depth", "au", "vert"),
    )
    sizes = tuple(mesh.shape[name] for name in ("depth", "au", "vert"))
    return jax.shard_map(
        functools.partial(per_device, sizes), mesh=mesh, in_specs=placed,
        out_specs=P("depth", "au", "vert"), check_vma=False,
    )
```
